32 devices in a mesh: parts: 2 (over y), region: 4 (over z), aux: 2 (over x), pno: 2 (over core).
Axes of the slice: x: 2, y: 2, z: 4, core: 2. Of those that a mesh axis runs over, the one named last changes fastest.
Arguments:
- three_index: bfloat16 [24, 3072, 256], P(('parts', 'region'), 'aux'), parts along dimension 0, may hold values from -1 to 1
- pno_maps: bfloat16 [128, 2, 256, 256], P(('parts', 'region'), None, None, 'pno'), parts along dimension 0, may hold values from -0.375 to 0.375
- amplitudes: bfloat16 [128, 256, 256], P(('parts', 'region'), 'pno'), parts along dimension 0, may hold values from -6 to 6
- pair_orbitals: int32 [128, 2], P('parts'), parts along dimension 0, may hold values from 0 to 11, as said below
- neighbours: int32 [128, 4], P(('parts', 'region')), parts along dimension 0, may hold values from 0 to 63, as said below
- couplings: float32 [128, 4], P(('parts', 'region')), parts along dimension 0, may hold values from -0.5 to 0.5
- pno_energies: float32 [128, 256], P(('parts', 'region')), parts along dimension 0, may hold values from 0.5 to 3
- occ_energies: float32 [24], P('parts'), parts along dimension 0, may hold values from -2 to -0.3
- pno_counts: int32 [128], P(('parts', 'region')), parts along dimension 0, may hold values from 64 to 256
Outputs:
- new_amplitudes: bfloat16 [128, 256, 256], P(('parts', 'region'), 'pno'), parts along dimension 0
- density: float32 [24, 256], P(('parts', 'region')), parts along dimension 0
The draws below stay inside these ranges and needn't reach their ends.
There are 2 independent parts, one for each index of `parts`. The reference program is written for one: setup_inputs(seed, part) draws one part's arguments, and reference() takes and returns one part's arrays. A program takes and returns all parts, laid end to end along the dimension named above; each array names one. Nothing has to cross between parts.
Inputs may be any that keep to these rules, and one draw needn't show every extreme that they name: `pair_orbitals`: pair p belongs to region p // 16; orbital o lies in region o // 3; a pair's first orbital lies in its own region; of one region's pairs at most 8 have their second orbital in any one region, and exactly 8 in some region. The neighbours of pair p belong to regions p // 16 - 1 to p // 16 + 1.
All inputs are finite; a program needn't handle non-finite values.
Results may differ from the reference program's by a relative error of at most 0.0065.
Values may be sent and summed in bfloat16 or wider, within the bound.
A program may use at most 128 MiB of HBM per device.

```python
import jax
import jax.numpy as jnp
from jax import lax

NAUX = 3072
NPNO = 256
NV = 256
NEIGHBOURS = 4
OCC_DEV = 3
PAIR_DEV = 16
OCC = 12
PAIRS = 64
CAP = 8


def draw_pair_orbitals(key, part):
    key = jax.random.fold_in(key, 11)
    regions = PAIRS // PAIR_DEV

    def one_device(device_key, owner_region):
        sub_keys = jax.random.split(device_key, 5)
        slot_pool = jnp.repeat(jnp.arange(regions, dtype=jnp.int32), CAP)
        shuffled = jax.random.permutation(sub_keys[0], slot_pool)
        first_source = jax.random.randint(sub_keys[1], (), 0, regions).astype(jnp.int32)
        order_score = (shuffled != first_source).astype(jnp.int32) * (regions * CAP) + jnp.arange(regions * CAP, dtype=jnp.int32)
        ordered = shuffled[jnp.argsort(order_score)]
        sources = jax.random.permutation(sub_keys[2], ordered[:PAIR_DEV])
        second_orb = sources * OCC_DEV + jax.random.randint(sub_keys[3], (PAIR_DEV,), 0, OCC_DEV).astype(jnp.int32)
        first_orb = owner_region * OCC_DEV + jax.random.randint(sub_keys[4], (PAIR_DEV,), 0, OCC_DEV).astype(jnp.int32)
        return jnp.stack([first_orb, second_orb], axis=1)
    device_keys = jax.random.split(key, regions)
    stacked = jax.vmap(one_device)(device_keys, jnp.arange(regions, dtype=jnp.int32))
    return stacked.reshape(PAIRS, 2).astype(jnp.int32)


def draw_neighbours(key, part):
    key = jax.random.fold_in(key, 23)
    regions = PAIRS // PAIR_DEV
    owner_region = jnp.arange(PAIRS, dtype=jnp.int32) // PAIR_DEV
    lower = jnp.maximum(owner_region - 1, 0)
    upper = jnp.minimum(owner_region + 1, regions - 1)
    column = jnp.arange(NEIGHBOURS, dtype=jnp.int32) % 4
    blocks = jnp.where(column[None, :] == 0, lower[:, None], jnp.where(column[None, :] == 1, upper[:, None], owner_region[:, None]))
    offsets = jax.random.randint(key, (PAIRS, NEIGHBOURS), 0, PAIR_DEV).astype(jnp.int32)
    return (blocks * PAIR_DEV + offsets).astype(jnp.int32)


def draw_pno_counts(key, part):
    key = jax.random.fold_in(key, 37)
    sub_keys = jax.random.split(key, 2)
    counts = jax.random.randint(sub_keys[0], (PAIRS,), NPNO // 4, NPNO + 1).astype(jnp.int32)
    widest = jax.random.randint(sub_keys[1], (), 0, PAIRS)
    return counts.at[widest].set(NPNO).astype(jnp.int32)


def block_levels(stream_key, extent, cuts, low, largest):
    def one(dim, parts):
        heights = jax.random.uniform(jax.random.fold_in(jax.random.fold_in(stream_key, 6), dim), (parts,), jnp.float32, low / len(cuts), largest / len(cuts))
        return jnp.repeat(jnp.exp(heights), extent[dim] // parts).reshape((-1,) + (1,) * (len(extent) - dim - 1))

    level = one(*cuts[0])
    for cut in cuts[1:]:
        level = level * one(*cut)
    return level


def centred(own_key, extent, spread, limit, cuts=(), kind=jnp.bfloat16):
    gain = block_levels(own_key, extent, cuts, -0.22, 0.18) if cuts else 1.0
    array = jax.random.normal(own_key, extent, jnp.float32) * spread * gain
    return jnp.minimum(jnp.maximum(array, -limit), limit).astype(kind)


def setup_inputs(seed: int = 0, part: int = 0) -> dict:
    splits = jax.random.split(jax.random.key(seed), 10)
    own_keys = jax.random.split(jax.random.fold_in(splits[9], part), 10)
    return {
        "three_index": centred(own_keys[0], (OCC, NAUX, NV), 0.135, 1.0, ((0, 4), (1, 2))),
        "pno_maps": centred(own_keys[1], (PAIRS, 2, NV, NPNO), NV ** -0.5, 0.375, ((0, 4), (3, 2))),
        "amplitudes": centred(own_keys[2], (PAIRS, NPNO, NPNO), 1.0, 6.0, ((0, 4), (1, 2))),
        "pair_orbitals": draw_pair_orbitals(jax.random.fold_in(jax.random.fold_in(splits[9], part), 71), part),
        "neighbours": draw_neighbours(jax.random.fold_in(jax.random.fold_in(splits[9], part), 71), part),
        "couplings": jnp.clip(jax.random.uniform(own_keys[5], (PAIRS, NEIGHBOURS), jnp.float32, -0.5, 0.5) * block_levels(own_keys[5], (PAIRS, NEIGHBOURS), ((0, 4),), -0.4, 0.0), -0.5, 0.5),
        "pno_energies": jnp.clip(0.5 + 2.5 * jax.random.uniform(own_keys[6], (PAIRS, NPNO), jnp.float32) ** block_levels(own_keys[6], (PAIRS, NPNO), ((0, 4),), -0.2, 0.2), 0.5, 3.0),
        "occ_energies": jnp.clip(jax.random.uniform(own_keys[7], (OCC,), jnp.float32, -2.0, -0.3), -2.0, -0.3),
        "pno_counts": draw_pno_counts(jax.random.fold_in(jax.random.fold_in(splits[9], part), 71), part),
    }


def reference(three_index, pno_maps, amplitudes, pair_orbitals, neighbours, couplings, pno_energies, occ_energies, pno_counts):
    first_orb = pair_orbitals[:, 0]
    second_orb = pair_orbitals[:, 1]

    def pair_terms(pair_index):
        left_rows = jnp.dot(three_index[first_orb[pair_index]], pno_maps[pair_index, 0], preferred_element_type=jnp.float32).astype(jnp.bfloat16)
        right_rows = jnp.dot(three_index[second_orb[pair_index]], pno_maps[pair_index, 1], preferred_element_type=jnp.float32).astype(jnp.bfloat16)
        return jnp.dot(left_rows.T, right_rows, preferred_element_type=jnp.float32)

    exchange = lax.map(pair_terms, jnp.arange(PAIRS, dtype=jnp.int32))
    coupling = jnp.zeros((PAIRS, NPNO, NPNO), jnp.float32)
    for neighbour in range(NEIGHBOURS):
        taken = amplitudes[neighbours[:, neighbour]].astype(jnp.float32)
        coupling = coupling + couplings[:, neighbour][:, None, None] * taken
    occupied = occ_energies[first_orb] + occ_energies[second_orb]
    denominator = (pno_energies[:, :, None] + pno_energies[:, None, :]) - occupied[:, None, None]
    index_range = jnp.arange(NPNO, dtype=jnp.int32)
    in_domain = (index_range[None, :, None] < pno_counts[:, None, None]) & (index_range[None, None, :] < pno_counts[:, None, None])
    update = jnp.where(in_domain, (coupling - exchange) / denominator, jnp.float32(0.0))
    weight = (jnp.sum(update * update, axis=2) / NPNO).astype(jnp.bfloat16)
    first_vec = jnp.einsum('pva,pa->pv', pno_maps[:, 0].astype(jnp.float32), weight.astype(jnp.float32))
    second_vec = jnp.einsum('pva,pa->pv', pno_maps[:, 1].astype(jnp.float32), weight.astype(jnp.float32))
    density = jnp.zeros((OCC, NV), jnp.float32).at[first_orb].add(first_vec).at[second_orb].add(second_vec)
    return update.astype(jnp.bfloat16), density
```

```python
import jax
import jax.numpy as jnp
from jax import lax
from jax.sharding import PartitionSpec as P


def with_halo(block, sides, width):
    for axis, dim in sides:
        count = lax.axis_size(axis)
        forward = [(i, i + 1) for i in range(count - 1)]
        backward = [(target, source) for source, target in forward]
        low = lax.ppermute(
            lax.slice_in_dim(block, block.shape[dim] - width, None, axis=dim), axis, forward
        )
        high = lax.ppermute(lax.slice_in_dim(block, 0, width, axis=dim), axis, backward)
        block = jnp.concatenate([low, block, high], axis=dim)
    return block


def body(
    three_index,
    pno_maps,
    amplitudes,
    pair_orbitals,
    neighbours,
    couplings,
    pno_energies,
    occ_energies,
    pno_counts,
):
    regions = lax.axis_size("region")
    region_index = lax.axis_index("region")
    pno_index = lax.axis_index("pno")
    occ_dev, aux_rows, virtuals = three_index.shape
    pair_dev = pno_maps.shape[0]
    columns = pno_maps.shape[3]
    width = amplitudes.shape[2]
    capacity = max(2, 2 * pair_dev // regions)
    partner = pair_orbitals[:, 1].reshape(regions, pair_dev)
    source = partner // occ_dev
    same_source = source[:, :, None] == source[:, None, :]
    positions = jnp.arange(pair_dev, dtype=jnp.int32)
    earlier = positions[None, :] < positions[:, None]
    slot_rank = jnp.sum(same_source & earlier[None], axis=2)
    first_orb = lax.dynamic_slice_in_dim(pair_orbitals[:, 0], region_index * pair_dev, pair_dev)
    my_partner = lax.dynamic_slice_in_dim(pair_orbitals[:, 1], region_index * pair_dev, pair_dev)
    my_rank = jnp.take(slot_rank, region_index, axis=0)
    slot_of_pair = my_partner // occ_dev * capacity + my_rank
    slot_ids = jnp.arange(regions * capacity, dtype=jnp.int32)
    match_out = slot_of_pair[None, :] == slot_ids[:, None]
    slot_pair = jnp.sum(jnp.where(match_out, positions[None, :], 0), axis=1)
    slot_used = jnp.any(match_out, axis=1)
    match_in = (source[:, None, :] == region_index) & (
        slot_rank[:, None, :] == jnp.arange(capacity, dtype=jnp.int32)[None, :, None]
    )
    local_orb = jnp.sum(
        jnp.where(match_in, partner[:, None, :] - region_index * occ_dev, 0), axis=2
    ).reshape(-1)
    local_used = jnp.any(match_in, axis=2).reshape(-1)
    first_maps = pno_maps[:, 0]
    second_maps = pno_maps[:, 1]
    regions_pno = lax.axis_size("pno")
    part_rows = aux_rows // regions_pno
    own_rows = lax.dynamic_slice_in_dim(three_index, pno_index * part_rows, part_rows, axis=1)
    all_rows = lax.all_gather(own_rows, "region", axis=0, tiled=True)
    gram = jnp.einsum("ikv,jkw->ijvw", own_rows, all_rows, preferred_element_type=jnp.float32)
    gram = gram.astype(jnp.bfloat16).reshape(-1, virtuals, virtuals)
    pair_gram = jnp.take(
        gram, (first_orb - region_index * occ_dev) * (regions * occ_dev) + my_partner, axis=0
    )
    full_maps = lax.all_gather(pno_maps, "pno", axis=3, tiled=True)
    half_way = jnp.einsum(
        "pva,pvw->paw", full_maps[:, 0], pair_gram, preferred_element_type=jnp.float32
    ).astype(jnp.bfloat16)
    partial_exchange = jnp.einsum(
        "paw,pwb->pab", half_way, full_maps[:, 1], preferred_element_type=jnp.float32
    )
    partial_exchange = lax.psum_scatter(partial_exchange, "pno", scatter_dimension=1, tiled=True)
    exchange = lax.psum(partial_exchange.astype(jnp.bfloat16), "aux").astype(jnp.float32)
    extended = with_halo(amplitudes, (("region", 0),), pair_dev)
    near_index = neighbours - (region_index - 1) * pair_dev
    coupling = jnp.zeros((pair_dev, columns, width), jnp.float32)
    for neighbour in range(neighbours.shape[1]):
        taken = jnp.take(extended, near_index[:, neighbour], axis=0)
        coupling = coupling + couplings[:, neighbour][:, None, None] * taken.astype(jnp.float32)
    own_energies = lax.dynamic_slice_in_dim(pno_energies, pno_index * columns, columns, 1)
    occupied = jnp.take(occ_energies, first_orb) + jnp.take(occ_energies, my_partner)
    denominator = own_energies[:, :, None] + pno_energies[:, None, :] - occupied[:, None, None]
    row_ids = pno_index * columns + jnp.arange(columns, dtype=jnp.int32)
    col_ids = jnp.arange(width, dtype=jnp.int32)
    in_domain = (row_ids[None, :, None] < pno_counts[:, None, None]) & (
        col_ids[None, None, :] < pno_counts[:, None, None]
    )
    update = jnp.where(in_domain, (coupling - exchange) / denominator, jnp.float32(0.0))
    weight = (jnp.sum(update * update, axis=2) / width).astype(jnp.bfloat16)
    first_vec = jnp.einsum("pva,pa->pv", first_maps, weight, preferred_element_type=jnp.float32)
    second_vec = jnp.einsum("pva,pa->pv", second_maps, weight, preferred_element_type=jnp.float32)
    orbital_ids = jnp.arange(occ_dev, dtype=jnp.int32)
    first_onehot = ((first_orb - region_index * occ_dev)[None, :] == orbital_ids[:, None]).astype(
        jnp.float32
    )
    density = jnp.dot(first_onehot, first_vec, precision=lax.Precision.HIGHEST)
    send_vecs = jnp.where(
        slot_used[:, None], jnp.take(second_vec, slot_pair, axis=0), jnp.float32(0.0)
    )
    received = lax.all_to_all(
        send_vecs.reshape(regions, capacity, virtuals).astype(jnp.bfloat16),
        "region",
        split_axis=0,
        concat_axis=0,
        tiled=True,
    ).astype(jnp.float32)
    second_onehot = ((local_orb[None, :] == orbital_ids[:, None]) & local_used[None, :]).astype(
        jnp.float32
    )
    density = density + jnp.dot(
        second_onehot,
        received.reshape(regions * capacity, virtuals),
        precision=lax.Precision.HIGHEST,
    )
    density = lax.psum(density, "pno")
    return (update.astype(jnp.bfloat16), density)


def solution(mesh):
    in_specs = (
        P(("parts", "region"), "aux", None),
        P(("parts", "region"), None, None, "pno"),
        P(("parts", "region"), "pno", None),
        P("parts", None),
        P(("parts", "region"), None),
        P(("parts", "region"), None),
        P(("parts", "region"), None),
        P("parts"),
        P(("parts", "region")),
    )
    out_specs = (P(("parts", "region"), "pno", None), P(("parts", "region"), None))
    return jax.shard_map(body, mesh=mesh, in_specs=in_specs, out_specs=out_specs, check_vma=False)
```

```python
import functools

import jax
import jax.numpy as jnp
from jax import lax
from jax.experimental import pallas as pl
from jax.experimental.pallas import tpu as pltpu
from jax.sharding import PartitionSpec as P

MESH = pl.DeviceIdType.MESH
F32 = jnp.float32
BF16 = jnp.bfloat16
CHUNK = 4


def exchange_kernel(
    regions,
    peers,
    first_ref,
    partner_ref,
    rows_ref,
    maps_ref,
    out_ref,
    own_t,
    edge_t,
    far_rows,
    gram,
    edge_gram,
    second_maps,
    first_t,
    partials,
    link_send,
    link_recv,
    core_send,
    core_recv,
    edge_send,
    maps_send,
    maps_recv,
    peer_send,
    peer_recv,
):
    occ, aux_rows, virtuals = rows_ref.shape
    pairs = maps_ref.shape[0]
    columns = maps_ref.shape[3]
    z = lax.axis_index("region")
    core = lax.axis_index("pno")
    mine = lax.axis_index("aux")
    part = aux_rows // 2
    half = virtuals // 2
    steps = (regions - 1) * occ
    slots = 2 * occ
    row_part = pl.ds(pl.multiple_of(core * part, part), part)
    row_rest = pl.ds(pl.multiple_of((1 - core) * part, part), part)
    gram_part = pl.ds(pl.multiple_of(core * half, half), half)
    gram_rest = pl.ds(pl.multiple_of((1 - core) * half, half), half)
    own_columns = pl.ds(pl.multiple_of(core * columns, columns), columns)
    sibling = {"pno": 1 - core}

    barrier = pltpu.get_barrier_semaphore()
    pl.semaphore_signal(barrier, inc=1, device_id=sibling, device_id_type=MESH)
    for k in range(1, peers):
        pl.semaphore_signal(
            barrier, inc=1, device_id={"aux": lax.rem(mine + k, peers)}, device_id_type=MESH
        )

    @pl.when(z > 0)
    def _():
        pl.semaphore_signal(barrier, inc=1, device_id={"region": z - 1}, device_id_type=MESH)

    @pl.when(z < regions - 1)
    def _():
        pl.semaphore_signal(barrier, inc=1, device_id={"region": z + 1}, device_id_type=MESH)

    neighbours = jnp.where(z > 0, 1, 0) + jnp.where(z < regions - 1, 1, 0)
    pl.semaphore_wait(barrier, peers + neighbours)

    def remote(src, dst, send, recv, device):
        return pltpu.make_async_remote_copy(
            src_ref=src,
            dst_ref=dst,
            send_sem=send,
            recv_sem=recv,
            device_id=device,
            device_id_type=MESH,
        )

    ahead = (z + 1, z - 1)
    ahead_exists = (z < regions - 1, z > 0)
    ahead_is_end = (z == regions - 2, z == 1)
    ahead_goes_on = (z < regions - 2, z > 1)
    at_end = (z == regions - 1, z == 0)

    def source(d, e):
        region = z - 1 - e // occ if d == 0 else z + 1 + e // occ
        return region, (region >= 0) & (region < regions), region * occ + lax.rem(e, occ)

    def own_copy(d, o):
        return remote(
            rows_ref.at[o, row_part],
            far_rows.at[z * occ + o, row_part],
            link_send.at[d, o],
            link_recv.at[d, o],
            {"region": ahead[d]},
        )

    def onward_copy(d, e, orbital):
        return remote(
            far_rows.at[orbital, row_part],
            far_rows.at[orbital, row_part],
            link_send.at[d, e + occ],
            link_recv.at[d, e + occ],
            {"region": ahead[d]},
        )

    def rows_to_core(d, e, orbital, which):
        return remote(
            far_rows.at[orbital, which],
            far_rows.at[orbital, which],
            core_send.at[d, e],
            core_recv.at[d, e],
            sibling,
        )

    def gram_to_core(d, e, orbital, which):
        return remote(
            gram.at[orbital, :, which],
            gram.at[orbital, :, which],
            core_send.at[d, e],
            core_recv.at[d, e],
            sibling,
        )

    def edge_copy(d, e, orbital):
        slot = lax.rem(e, slots)
        return remote(
            edge_gram.at[slot, :, gram_part],
            gram.at[orbital, :, gram_part],
            edge_send.at[slot],
            link_recv.at[d, e + occ],
            {"region": ahead[d]},
        )

    def maps_copy():
        return remote(
            maps_ref.at[:, 1],
            second_maps.at[:, :, own_columns],
            maps_send,
            maps_recv,
            sibling,
        )

    for d in range(2):

        @pl.when(ahead_exists[d])
        def _(d=d):
            for o in range(occ):
                own_copy(d, o).start()

    maps_copy().start()
    for o in range(occ):
        own_t[o] = rows_ref[o].T

    def own_gram(o, carry):
        for i in range(occ):
            gram[z * occ + o, i] = jnp.dot(
                own_t[i], rows_ref[o], preferred_element_type=F32
            ).astype(BF16)
        return carry

    lax.fori_loop(0, occ, own_gram, 0)

    def prepare_maps(p, carry):
        first_t[p] = maps_ref[p, 0].T
        second_maps[p, :, own_columns] = maps_ref[p, 1]
        return carry

    lax.fori_loop(0, pairs, prepare_maps, 0)

    def edge_step(d, e):
        region, valid, orbital = source(d, e)

        @pl.when(valid)
        def _():
            @pl.when(e >= slots)
            def _():
                edge_copy(d, e, orbital).wait_send()

            for i in range(occ):
                edge_gram[lax.rem(e, slots), i] = jnp.dot(
                    edge_t[i], far_rows[orbital], preferred_element_type=F32
                ).astype(BF16)
            edge_copy(d, e, orbital).start()

    def step(e, carry):
        for d in range(2):
            region, valid, orbital = source(d, e)
            is_gram = at_end[d] & (e >= occ)

            @pl.when(valid & jnp.logical_not(is_gram))
            def _(d=d, orbital=orbital):
                onward_copy(d, e - occ, orbital).wait_recv()
                rows_to_core(d, e, orbital, row_part).start()

                @pl.when(ahead_goes_on[d])
                def _():
                    onward_copy(d, e, orbital).start()

            @pl.when(valid & is_gram)
            def _(d=d, orbital=orbital):
                remote(
                    gram.at[orbital, :, gram_part],
                    gram.at[orbital, :, gram_part],
                    link_send.at[d, e],
                    link_recv.at[d, e],
                    sibling,
                ).wait_recv()
                gram_to_core(d, e, orbital, gram_part).start()

        for d in range(2):
            region, valid, orbital = source(d, e)
            is_gram = at_end[d] & (e >= occ)

            @pl.when(valid & jnp.logical_not(is_gram))
            def _(d=d, orbital=orbital):
                rows_to_core(d, e, orbital, row_rest).wait_recv()

                @pl.when(ahead_is_end[d] & (e >= occ))
                def _():
                    edge_step(d, e)

                for i in range(occ):
                    gram[orbital, i] = jnp.dot(
                        own_t[i], far_rows[orbital], preferred_element_type=F32
                    ).astype(BF16)

            @pl.when(valid & is_gram)
            def _(d=d, orbital=orbital):
                gram_to_core(d, e, orbital, gram_rest).wait_recv()

        for d in range(2):

            @pl.when(ahead_is_end[d] & (e == occ - 1))
            def _(d=d):
                for o in range(occ):
                    edge_t[o] = far_rows[ahead[d] * occ + o].T

                def first_edges(k, inner):
                    edge_step(d, k)
                    return inner

                lax.fori_loop(0, occ, first_edges, 0)

        return carry

    lax.fori_loop(0, steps, step, 0)

    remote(
        maps_ref.at[:, 1],
        second_maps.at[:, :, pl.ds(pl.multiple_of((1 - core) * columns, columns), columns)],
        maps_send,
        maps_recv,
        sibling,
    ).wait_recv()

    def peer_copy(k, c):
        block = pl.ds(c * CHUNK, CHUNK)
        return remote(
            partials.at[mine, block],
            partials.at[mine, block],
            peer_send.at[k - 1, c],
            peer_recv.at[k - 1, c],
            {"aux": lax.rem(mine + k, peers)},
        )

    def project(c, carry):
        for q in range(CHUNK):
            p = c * CHUNK + q
            matrix = gram[partner_ref[p], first_ref[p]]
            turned = jnp.dot(first_t[p], matrix, preferred_element_type=F32).astype(BF16)
            block = jnp.dot(turned, second_maps[p], preferred_element_type=F32)
            partials[mine, p] = block.astype(BF16)
        for k in range(1, peers):
            peer_copy(k, c).start()
        return carry

    lax.fori_loop(0, pairs // CHUNK, project, 0)

    def drain(e, carry):
        for d in range(2):
            region, valid, orbital = source(d, e)
            is_gram = at_end[d] & (e >= occ)

            @pl.when(valid & jnp.logical_not(is_gram))
            def _(d=d, orbital=orbital):
                rows_to_core(d, e, orbital, row_part).wait_send()

                @pl.when(ahead_goes_on[d])
                def _():
                    onward_copy(d, e, orbital).wait_send()

                @pl.when(
                    ahead_is_end[d] & ((e >= (regions - 2) * occ - slots))
                )
                def _():
                    edge_copy(d, e, orbital).wait_send()

            @pl.when(valid & is_gram)
            def _(d=d, orbital=orbital):
                gram_to_core(d, e, orbital, gram_part).wait_send()

        return carry

    lax.fori_loop(0, steps, drain, 0)
    for d in range(2):

        @pl.when(ahead_exists[d])
        def _(d=d):
            for o in range(occ):
                own_copy(d, o).wait_send()

    maps_copy().wait_send()

    def collect(c, carry):
        for k in range(1, peers):
            origin = lax.rem(mine - k + peers, peers)
            block = pl.ds(c * CHUNK, CHUNK)
            peer_copy(k, c).wait_send()
            remote(
                partials.at[origin, block],
                partials.at[origin, block],
                peer_send.at[k - 1, c],
                peer_recv.at[k - 1, c],
                {"aux": lax.rem(mine + k, peers)},
            ).wait_recv()
        for q in range(CHUNK):
            p = c * CHUNK + q
            total = partials[0, p].astype(F32)
            for k in range(1, peers):
                total = total + partials[k, p].astype(F32)
            out_ref[p] = total
        return carry

    lax.fori_loop(0, pairs // CHUNK, collect, 0)


def exchange_call(three_index, pno_maps, first_local, partner):
    regions = lax.axis_size("region")
    peers = lax.axis_size("aux")
    occ, aux_rows, virtuals = three_index.shape
    pairs, _, _, columns = pno_maps.shape
    width = columns * lax.axis_size("pno")
    orbitals = regions * occ
    steps = (regions - 1) * occ
    smem = pl.BlockSpec(memory_space=pltpu.SMEM)
    vmem = pl.BlockSpec(memory_space=pltpu.VMEM)
    dma = pltpu.SemaphoreType.DMA
    return pl.pallas_call(
        functools.partial(exchange_kernel, regions, peers),
        out_shape=jax.ShapeDtypeStruct((pairs, columns, width), F32),
        in_specs=[smem, smem, vmem, vmem],
        out_specs=vmem,
        scratch_shapes=[
            pltpu.VMEM((occ, virtuals, aux_rows), BF16),
            pltpu.VMEM((occ, virtuals, aux_rows), BF16),
            pltpu.VMEM((orbitals, aux_rows, virtuals), BF16),
            pltpu.VMEM((orbitals, occ, virtuals, virtuals), BF16),
            pltpu.VMEM((2 * occ, occ, virtuals, virtuals), BF16),
            pltpu.VMEM((pairs, virtuals, width), BF16),
            pltpu.VMEM((pairs, columns, virtuals), BF16),
            pltpu.VMEM((peers, pairs, columns, width), BF16),
            dma((2, steps)),
            dma((2, steps)),
            dma((2, steps)),
            dma((2, steps)),
            dma((2 * occ,)),
            dma,
            dma,
            dma((peers - 1, pairs // CHUNK)),
            dma((peers - 1, pairs // CHUNK)),
        ],
        compiler_params=pltpu.CompilerParams(
            collective_id=0, has_side_effects=True, vmem_limit_bytes=58 * 2**20
        ),
        cost_estimate=pl.CostEstimate(
            flops=10**10, bytes_accessed=150 * 10**6, transcendentals=0
        ),
        name="exchange",
    )(first_local, partner, three_index, pno_maps)


def update_kernel(
    near_ref,
    couplings_ref,
    occupied_ref,
    counts_ref,
    first_ref,
    partner_ref,
    start_ref,
    exchange_ref,
    below_ref,
    own_ref,
    above_ref,
    own_energies_ref,
    energies_ref,
    maps_ref,
    new_ref,
    density_ref,
    nearby,
    sems,
):
    pairs, columns, width = exchange_ref.shape
    copies = [
        pltpu.make_async_copy(ref, nearby.at[pl.ds(k * pairs, pairs)], sems.at[k])
        for k, ref in enumerate((below_ref, own_ref, above_ref))
    ]
    for copy in copies:
        copy.start()
    density_ref[...] = jnp.zeros_like(density_ref)
    start = start_ref[0]
    row_ids = start + lax.broadcasted_iota(jnp.int32, (columns, width), 0)
    col_ids = lax.broadcasted_iota(jnp.int32, (columns, width), 1)
    last_ids = jnp.maximum(row_ids, col_ids)
    for copy in copies:
        copy.wait()

    def one(p, carry):
        coupling = jnp.zeros((columns, width), F32)
        for n in range(near_ref.shape[1]):
            coupling = coupling + couplings_ref[p, n] * nearby[near_ref[p, n]].astype(F32)
        row_energy = jnp.broadcast_to(own_energies_ref[pl.ds(p, 1)], (width, columns)).T
        denominator = row_energy + energies_ref[pl.ds(p, 1)] - occupied_ref[p]
        update = jnp.where(
            last_ids < counts_ref[p], (coupling - exchange_ref[p]) / denominator, 0.0
        )
        new_ref[p] = update.astype(BF16)
        weight = jnp.sum(update * update, axis=1, keepdims=True) / width
        weight = jnp.broadcast_to(weight, (columns, columns)).T[0:8].astype(BF16)
        contract = (((1,), (1,)), ((), ()))
        for which, orbital in ((0, first_ref[p]), (1, partner_ref[p])):
            vec = lax.dot_general(
                weight, maps_ref[p, which], contract, preferred_element_type=F32
            )
            density_ref[pl.ds(orbital, 1)] += vec[0:1]
        return carry

    lax.fori_loop(0, pairs, one, 0)


def body(
    three_index,
    pno_maps,
    amplitudes,
    pair_orbitals,
    neighbours,
    couplings,
    pno_energies,
    occ_energies,
    pno_counts,
):
    regions = lax.axis_size("region")
    region_index = lax.axis_index("region")
    pno_index = lax.axis_index("pno")
    occ_dev, aux_rows, virtuals = three_index.shape
    pair_dev, _, _, columns = pno_maps.shape
    width = amplitudes.shape[2]
    mine = lax.dynamic_slice_in_dim(pair_orbitals, region_index * pair_dev, pair_dev)
    first_orb, partner = mine[:, 0], mine[:, 1]
    forward = [(i, i + 1) for i in range(regions - 1)]
    backward = [(target, origin) for origin, target in forward]
    below = lax.ppermute(amplitudes, "region", forward)
    above = lax.ppermute(amplitudes, "region", backward)
    exchange = exchange_call(three_index, pno_maps, first_orb - region_index * occ_dev, partner)
    near = neighbours - (region_index - 1) * pair_dev
    own_energies = lax.dynamic_slice_in_dim(pno_energies, pno_index * columns, columns, 1)
    occupied = jnp.take(occ_energies, first_orb) + jnp.take(occ_energies, partner)
    smem = pl.BlockSpec(memory_space=pltpu.SMEM)
    vmem = pl.BlockSpec(memory_space=pltpu.VMEM)
    anywhere = pl.BlockSpec(memory_space=pl.ANY)
    update, density = pl.pallas_call(
        update_kernel,
        out_shape=(
            jax.ShapeDtypeStruct((pair_dev, columns, width), BF16),
            jax.ShapeDtypeStruct((regions * occ_dev, virtuals), F32),
        ),
        in_specs=[smem] * 7 + [vmem] + [anywhere] * 3 + [vmem] * 3,
        out_specs=(vmem, vmem),
        scratch_shapes=[
            pltpu.VMEM((3 * pair_dev, columns, width), BF16),
            pltpu.SemaphoreType.DMA((3,)),
        ],
        compiler_params=pltpu.CompilerParams(vmem_limit_bytes=40 * 2**20),
        name="update",
    )(
        near,
        couplings,
        occupied,
        pno_counts,
        first_orb,
        partner,
        (pno_index * columns).reshape(1).astype(jnp.int32),
        exchange,
        below,
        amplitudes,
        above,
        own_energies,
        pno_energies,
        pno_maps,
    )
    density = lax.psum(density, ("region", "pno"))
    density = lax.dynamic_slice_in_dim(density, region_index * occ_dev, occ_dev)
    return (update, density)


def solution(mesh):
    in_specs = (
        P(("parts", "region"), "aux", None),
        P(("parts", "region"), None, None, "pno"),
        P(("parts", "region"), "pno", None),
        P("parts", None),
        P(("parts", "region"), None),
        P(("parts", "region"), None),
        P(("parts", "region"), None),
        P("parts"),
        P(("parts", "region")),
    )
    out_specs = (P(("parts", "region"), "pno", None), P(("parts", "region"), None))
    return jax.shard_map(body, mesh=mesh, in_specs=in_specs, out_specs=out_specs, check_vma=False)
```

```python
import functools

import jax
import jax.numpy as jnp
from jax import lax
from jax.experimental import pallas as pl
from jax.experimental.pallas import tpu as pltpu
from jax.sharding import PartitionSpec as P

MESH = pl.DeviceIdType.MESH
F32 = jnp.float32
BF16 = jnp.bfloat16
CHUNK = 4


def exchange_kernel(
    regions,
    peers,
    orbitals_ref,
    near_ref,
    couplings_ref,
    occupied_ref,
    counts_ref,
    rows_ref,
    maps_ref,
    energies_ref,
    amplitudes_ref,
    new_ref,
    density_ref,
    own_t,
    edge_t,
    far_rows,
    gram,
    edge_gram,
    second_maps,
    first_t,
    partials,
    nearby,
    spread,
    gathered,
    link_send,
    link_recv,
    core_send,
    core_recv,
    edge_send,
    maps_send,
    maps_recv,
    peer_send,
    peer_recv,
    own_sem,
    halo_send,
    halo_recv,
    share_send,
    share_recv,
    spread_send,
    spread_recv,
):
    occ, aux_rows, virtuals = rows_ref.shape
    pairs = maps_ref.shape[0]
    columns = maps_ref.shape[3]
    z = lax.axis_index("region")
    core = lax.axis_index("pno")
    mine = lax.axis_index("aux")
    part = aux_rows // 2
    half = virtuals // 2
    steps = (regions - 1) * occ
    slots = 2 * occ
    row_part = pl.ds(pl.multiple_of(core * part, part), part)
    row_rest = pl.ds(pl.multiple_of((1 - core) * part, part), part)
    gram_part = pl.ds(pl.multiple_of(core * half, half), half)
    gram_rest = pl.ds(pl.multiple_of((1 - core) * half, half), half)
    own_columns = pl.ds(pl.multiple_of(core * columns, columns), columns)
    sibling = {"pno": 1 - core}

    members = 2 * regions
    place = 2 * z + core
    share = pairs // peers
    width = 2 * columns

    barrier = pltpu.get_barrier_semaphore()
    for k in range(1, members):
        target = lax.rem(place + k, members)
        pl.semaphore_signal(
            barrier,
            inc=1,
            device_id={"region": target // 2, "pno": lax.rem(target, 2)},
            device_id_type=MESH,
        )
    for k in range(1, peers):
        pl.semaphore_signal(
            barrier, inc=1, device_id={"aux": lax.rem(mine + k, peers)}, device_id_type=MESH
        )
    own_amplitudes = pltpu.make_async_copy(
        amplitudes_ref, nearby.at[pl.ds(pairs, pairs)], own_sem
    )
    own_amplitudes.start()
    pl.semaphore_wait(barrier, members - 1 + peers - 1)

    def remote(src, dst, send, recv, device):
        return pltpu.make_async_remote_copy(
            src_ref=src,
            dst_ref=dst,
            send_sem=send,
            recv_sem=recv,
            device_id=device,
            device_id_type=MESH,
        )

    ahead = (z + 1, z - 1)
    ahead_exists = (z < regions - 1, z > 0)
    ahead_is_end = (z == regions - 2, z == 1)
    ahead_goes_on = (z < regions - 2, z > 1)
    at_end = (z == regions - 1, z == 0)

    def source(d, e):
        region = z - 1 - e // occ if d == 0 else z + 1 + e // occ
        return region, (region >= 0) & (region < regions), region * occ + lax.rem(e, occ)

    def own_copy(d, o):
        return remote(
            rows_ref.at[o, row_part],
            far_rows.at[z * occ + o, row_part],
            link_send.at[d, o],
            link_recv.at[d, o],
            {"region": ahead[d]},
        )

    def onward_copy(d, e, orbital):
        return remote(
            far_rows.at[orbital, row_part],
            far_rows.at[orbital, row_part],
            link_send.at[d, e + occ],
            link_recv.at[d, e + occ],
            {"region": ahead[d]},
        )

    def rows_to_core(d, e, orbital, which):
        return remote(
            far_rows.at[orbital, which],
            far_rows.at[orbital, which],
            core_send.at[d, e],
            core_recv.at[d, e],
            sibling,
        )

    def gram_to_core(d, e, orbital, which):
        return remote(
            gram.at[orbital, :, which],
            gram.at[orbital, :, which],
            core_send.at[d, e],
            core_recv.at[d, e],
            sibling,
        )

    def edge_copy(d, e, orbital):
        slot = lax.rem(e, slots)
        return remote(
            edge_gram.at[slot, :, gram_part],
            gram.at[orbital, :, gram_part],
            edge_send.at[slot],
            link_recv.at[d, e + occ],
            {"region": ahead[d]},
        )

    def maps_copy():
        return remote(
            maps_ref.at[:, 1],
            second_maps.at[:, :, own_columns],
            maps_send,
            maps_recv,
            sibling,
        )

    def halo_copy(d):
        return remote(
            nearby.at[pl.ds(pairs + mine * share, share)],
            nearby.at[pl.ds((0 if d == 0 else 2) * pairs + mine * share, share)],
            halo_send.at[d],
            halo_recv.at[d],
            {"region": ahead[d]},
        )

    def share_copy(d, k, origin):
        block = nearby.at[pl.ds((0 if d == 0 else 2) * pairs + origin * share, share)]
        return remote(
            block,
            block,
            share_send.at[d, k - 1],
            share_recv.at[d, k - 1],
            {"aux": lax.rem(mine + k, peers)},
        )

    behind_exists = (z > 0, z < regions - 1)

    for d in range(2):

        @pl.when(ahead_exists[d])
        def _(d=d):
            for o in range(occ):
                own_copy(d, o).start()

        @pl.when(jnp.logical_not(behind_exists[d]))
        def _(d=d):
            nearby[pl.ds((0 if d == 0 else 2) * pairs, pairs)] = jnp.zeros(
                (pairs, columns, width), BF16
            )

    maps_copy().start()
    for o in range(occ):
        own_t[o] = rows_ref[o].T

    def own_gram(o, carry):
        for i in range(occ):
            gram[z * occ + o, i] = jnp.dot(
                own_t[i], rows_ref[o], preferred_element_type=F32
            ).astype(BF16)
        return carry

    lax.fori_loop(0, occ, own_gram, 0)

    def prepare_maps(p, carry):
        first_t[p] = maps_ref[p, 0].T
        second_maps[p, :, own_columns] = maps_ref[p, 1]
        return carry

    lax.fori_loop(0, pairs, prepare_maps, 0)
    own_amplitudes.wait()

    def edge_step(d, e):
        region, valid, orbital = source(d, e)

        @pl.when(valid)
        def _():
            @pl.when(e >= slots)
            def _():
                edge_copy(d, e, orbital).wait_send()

            for i in range(occ):
                edge_gram[lax.rem(e, slots), i] = jnp.dot(
                    edge_t[i], far_rows[orbital], preferred_element_type=F32
                ).astype(BF16)
            edge_copy(d, e, orbital).start()

    def step(e, carry):
        for d in range(2):
            region, valid, orbital = source(d, e)
            is_gram = at_end[d] & (e >= occ)

            @pl.when(valid & jnp.logical_not(is_gram))
            def _(d=d, orbital=orbital):
                onward_copy(d, e - occ, orbital).wait_recv()
                rows_to_core(d, e, orbital, row_part).start()

                @pl.when(ahead_goes_on[d])
                def _():
                    onward_copy(d, e, orbital).start()

            @pl.when(valid & is_gram)
            def _(d=d, orbital=orbital):
                remote(
                    gram.at[orbital, :, gram_part],
                    gram.at[orbital, :, gram_part],
                    link_send.at[d, e],
                    link_recv.at[d, e],
                    sibling,
                ).wait_recv()
                gram_to_core(d, e, orbital, gram_part).start()

        for d in range(2):

            @pl.when(ahead_exists[d] & (e == occ))
            def _(d=d):
                halo_copy(d).start()

        for d in range(2):
            region, valid, orbital = source(d, e)
            is_gram = at_end[d] & (e >= occ)

            @pl.when(valid & jnp.logical_not(is_gram))
            def _(d=d, orbital=orbital):
                rows_to_core(d, e, orbital, row_rest).wait_recv()

                @pl.when(ahead_is_end[d] & (e >= occ))
                def _():
                    edge_step(d, e)

                for i in range(occ):
                    gram[orbital, i] = jnp.dot(
                        own_t[i], far_rows[orbital], preferred_element_type=F32
                    ).astype(BF16)

            @pl.when(valid & is_gram)
            def _(d=d, orbital=orbital):
                gram_to_core(d, e, orbital, gram_rest).wait_recv()

        for d in range(2):

            @pl.when(ahead_is_end[d] & (e == occ - 1))
            def _(d=d):
                for o in range(occ):
                    edge_t[o] = far_rows[ahead[d] * occ + o].T

                def first_edges(k, inner):
                    edge_step(d, k)
                    return inner

                lax.fori_loop(0, occ, first_edges, 0)

        return carry

    lax.fori_loop(0, steps, step, 0)

    remote(
        maps_ref.at[:, 1],
        second_maps.at[:, :, pl.ds(pl.multiple_of((1 - core) * columns, columns), columns)],
        maps_send,
        maps_recv,
        sibling,
    ).wait_recv()

    def peer_copy(k, c):
        block = pl.ds(c * CHUNK, CHUNK)
        return remote(
            partials.at[mine, block],
            partials.at[mine, block],
            peer_send.at[k - 1, c],
            peer_recv.at[k - 1, c],
            {"aux": lax.rem(mine + k, peers)},
        )

    def project(c, carry):
        for q in range(CHUNK):
            p = c * CHUNK + q
            first = jnp.clip(orbitals_ref[z * pairs + p, 0] - z * occ, 0, occ - 1)
            matrix = gram[orbitals_ref[z * pairs + p, 1], first]
            turned = jnp.dot(first_t[p], matrix, preferred_element_type=F32).astype(BF16)
            block = jnp.dot(turned, second_maps[p], preferred_element_type=F32)
            partials[mine, p] = block.astype(BF16)
        for k in range(1, peers):
            peer_copy(k, c).start()
        return carry

    lax.fori_loop(0, pairs // CHUNK, project, 0)

    for d in range(2):

        @pl.when(behind_exists[d])
        def _(d=d):
            block = nearby.at[pl.ds((0 if d == 0 else 2) * pairs + mine * share, share)]
            remote(block, block, halo_send.at[d], halo_recv.at[d], sibling).wait_recv()
            for k in range(1, peers):
                share_copy(d, k, mine).start()

    for d in range(2):

        @pl.when(behind_exists[d])
        def _(d=d):
            for k in range(1, peers):
                share_copy(d, k, mine).wait_send()
                share_copy(d, k, lax.rem(mine - k + peers, peers)).wait_recv()

    row_ids = core * columns + lax.broadcasted_iota(jnp.int32, (columns, width), 0)
    col_ids = lax.broadcasted_iota(jnp.int32, (columns, width), 1)
    last_ids = jnp.maximum(row_ids, col_ids)
    orbital_ids = lax.broadcasted_iota(
        jnp.int32, spread.shape, 0
    ) * occ + lax.broadcasted_iota(jnp.int32, spread.shape, 1)
    held = lax.broadcasted_iota(jnp.int32, spread.shape, 1) < occ
    orbital_ids = jnp.where(held, orbital_ids, -1)
    spread[...] = jnp.zeros_like(spread)
    contract = (((1,), (1,)), ((), ()))

    def collect(c, carry):
        for k in range(1, peers):
            origin = lax.rem(mine - k + peers, peers)
            block = pl.ds(c * CHUNK, CHUNK)
            remote(
                partials.at[origin, block],
                partials.at[origin, block],
                peer_send.at[k - 1, c],
                peer_recv.at[k - 1, c],
                {"aux": lax.rem(mine + k, peers)},
            ).wait_recv()
        for q in range(CHUNK):
            p = c * CHUNK + q
            exchange = partials[0, p].astype(F32)
            for k in range(1, peers):
                exchange = exchange + partials[k, p].astype(F32)
            coupling = jnp.zeros((columns, width), F32)
            for n in range(near_ref.shape[1]):
                taken = nearby[jnp.clip(near_ref[p, n] - (z - 1) * pairs, 0, 3 * pairs - 1)]
                coupling = coupling + couplings_ref[p, n] * taken.astype(F32)
            first = orbitals_ref[z * pairs + p, 0]
            second = orbitals_ref[z * pairs + p, 1]
            occupied = occupied_ref[first] + occupied_ref[second]
            energies = energies_ref[pl.ds(p, 1)]
            own_energies = jnp.where(core == 0, energies[:, :columns], energies[:, columns:])
            row_energy = jnp.broadcast_to(own_energies, (width, columns)).T
            denominator = row_energy + energies - occupied
            update = jnp.where(
                last_ids < counts_ref[p], (coupling - exchange) / denominator, 0.0
            )
            new_ref[p] = update.astype(BF16)
            weight = jnp.sum(update * update, axis=1, keepdims=True) / width
            weight = jnp.broadcast_to(weight, (columns, columns)).T[0:8].astype(BF16)
            for which, orbital in ((0, first), (1, second)):
                vec = lax.dot_general(
                    weight, maps_ref[p, which], contract, preferred_element_type=F32
                )
                spread[...] += jnp.where(orbital_ids == orbital, vec[None], 0.0)
        return carry

    lax.fori_loop(0, pairs // CHUNK, collect, 0)

    def spread_copy(k):
        target = lax.rem(place + k, members)
        return remote(
            spread.at[target // 2],
            gathered.at[place],
            spread_send.at[k - 1],
            spread_recv.at[k - 1],
            {"region": target // 2, "pno": lax.rem(target, 2)},
        )

    for k in range(1, members):
        spread_copy(k).start()
    gathered[place] = spread[z]

    def drain(e, carry):
        for d in range(2):
            region, valid, orbital = source(d, e)
            is_gram = at_end[d] & (e >= occ)

            @pl.when(valid & jnp.logical_not(is_gram))
            def _(d=d, orbital=orbital):
                rows_to_core(d, e, orbital, row_part).wait_send()

                @pl.when(ahead_goes_on[d])
                def _():
                    onward_copy(d, e, orbital).wait_send()

                @pl.when(
                    ahead_is_end[d] & ((e >= (regions - 2) * occ - slots))
                )
                def _():
                    edge_copy(d, e, orbital).wait_send()

            @pl.when(valid & is_gram)
            def _(d=d, orbital=orbital):
                gram_to_core(d, e, orbital, gram_part).wait_send()

        return carry

    lax.fori_loop(0, steps, drain, 0)
    for d in range(2):

        @pl.when(ahead_exists[d])
        def _(d=d):
            for o in range(occ):
                own_copy(d, o).wait_send()

    maps_copy().wait_send()

    for d in range(2):

        @pl.when(ahead_exists[d])
        def _(d=d):
            halo_copy(d).wait_send()

    def drain_peers(c, carry):
        for k in range(1, peers):
            peer_copy(k, c).wait_send()
        return carry

    lax.fori_loop(0, pairs // CHUNK, drain_peers, 0)
    for k in range(1, members):
        spread_copy(k).wait_send()
        origin = lax.rem(place - k + members, members)
        remote(
            gathered.at[origin],
            gathered.at[origin],
            spread_send.at[k - 1],
            spread_recv.at[k - 1],
            sibling,
        ).wait_recv()
    total = gathered[0]
    for k in range(1, members):
        total = total + gathered[k]
    density_ref[...] = total[0:occ]


def body(
    three_index,
    pno_maps,
    amplitudes,
    pair_orbitals,
    neighbours,
    couplings,
    pno_energies,
    occ_energies,
    pno_counts,
):
    regions = lax.axis_size("region")
    peers = lax.axis_size("aux")
    occ, aux_rows, virtuals = three_index.shape
    pairs, _, _, columns = pno_maps.shape
    width = columns * lax.axis_size("pno")
    orbitals = regions * occ
    steps = (regions - 1) * occ
    smem = pl.BlockSpec(memory_space=pltpu.SMEM)
    vmem = pl.BlockSpec(memory_space=pltpu.VMEM)
    anywhere = pl.BlockSpec(memory_space=pl.ANY)
    dma = pltpu.SemaphoreType.DMA
    return pl.pallas_call(
        functools.partial(exchange_kernel, regions, peers),
        out_shape=(
            jax.ShapeDtypeStruct((pairs, columns, width), BF16),
            jax.ShapeDtypeStruct((occ, virtuals), F32),
        ),
        in_specs=[smem] * 5 + [vmem] * 3 + [anywhere],
        out_specs=(vmem, vmem),
        scratch_shapes=[
            pltpu.VMEM((occ, virtuals, aux_rows), BF16),
            pltpu.VMEM((occ, virtuals, aux_rows), BF16),
            pltpu.VMEM((orbitals, aux_rows, virtuals), BF16),
            pltpu.VMEM((orbitals, occ, virtuals, virtuals), BF16),
            pltpu.VMEM((2 * occ, occ, virtuals, virtuals), BF16),
            pltpu.VMEM((pairs, virtuals, width), BF16),
            pltpu.VMEM((pairs, columns, virtuals), BF16),
            pltpu.VMEM((peers, pairs, columns, width), BF16),
            pltpu.VMEM((3 * pairs, columns, width), BF16),
            pltpu.VMEM((regions, 8, virtuals), F32),
            pltpu.VMEM((2 * regions, 8, virtuals), F32),
            dma((2, steps)),
            dma((2, steps)),
            dma((2, steps)),
            dma((2, steps)),
            dma((2 * occ,)),
            dma,
            dma,
            dma((peers - 1, pairs // CHUNK)),
            dma((peers - 1, pairs // CHUNK)),
            dma,
            dma((2,)),
            dma((2,)),
            dma((2, peers - 1)),
            dma((2, peers - 1)),
            dma((2 * regions - 1,)),
            dma((2 * regions - 1,)),
        ],
        compiler_params=pltpu.CompilerParams(
            collective_id=0, has_side_effects=True, vmem_limit_bytes=58 * 2**20
        ),
        cost_estimate=pl.CostEstimate(
            flops=10**10, bytes_accessed=150 * 10**6, transcendentals=0
        ),
        name="update",
    )(
        pair_orbitals,
        neighbours,
        couplings,
        occ_energies,
        pno_counts,
        three_index,
        pno_maps,
        pno_energies,
        amplitudes,
    )


def solution(mesh):
    in_specs = (
        P(("parts", "region"), "aux", None),
        P(("parts", "region"), None, None, "pno"),
        P(("parts", "region"), "pno", None),
        P("parts", None),
        P(("parts", "region"), None),
        P(("parts", "region"), None),
        P(("parts", "region"), None),
        P("parts"),
        P(("parts", "region")),
    )
    out_specs = (P(("parts", "region"), "pno", None), P(("parts", "region"), None))
    return jax.shard_map(body, mesh=mesh, in_specs=in_specs, out_specs=out_specs, check_vma=False)
```

```python
import functools

import jax
import jax.numpy as jnp
from jax import lax
from jax.experimental import pallas as pl
from jax.experimental.pallas import tpu as pltpu
from jax.sharding import PartitionSpec as P

MESH = pl.DeviceIdType.MESH
F32 = jnp.float32
BF16 = jnp.bfloat16
CHUNK = 4
DEPTH = 2
HALO_STEP = 0
SHARE_STEP = 2


def exchange_kernel(
    regions,
    peers,
    whole_ref,
    occupied_ref,
    counts_ref,
    couplings_ref,
    rows_ref,
    maps_ref,
    energies_ref,
    amplitudes_ref,
    new_ref,
    density_ref,
    own_t,
    edge_t,
    far_rows,
    gram,
    edge_gram,
    second_maps,
    first_t,
    partials,
    nearby,
    spread,
    gathered,
    link_send,
    link_recv,
    core_send,
    core_recv,
    edge_send,
    maps_send,
    maps_recv,
    peer_send,
    peer_recv,
    own_sem,
    halo_send,
    halo_recv,
    share_send,
    share_recv,
    spread_send,
    spread_recv,
):
    occ, aux_rows, virtuals = rows_ref.shape
    pairs = maps_ref.shape[0]
    columns = maps_ref.shape[3]
    z = lax.axis_index("region")
    core = lax.axis_index("pno")
    mine = lax.axis_index("aux")
    part = aux_rows // 2
    half = virtuals // 2
    steps = (regions - 1) * occ
    slots = 2 * occ
    row_part = pl.ds(pl.multiple_of(core * part, part), part)
    row_rest = pl.ds(pl.multiple_of((1 - core) * part, part), part)
    gram_part = pl.ds(pl.multiple_of(core * half, half), half)
    gram_rest = pl.ds(pl.multiple_of((1 - core) * half, half), half)
    own_columns = pl.ds(pl.multiple_of(core * columns, columns), columns)
    sibling = {"pno": 1 - core}

    members = 2 * regions
    place = 2 * z + core
    share = pairs // peers
    width = 2 * columns

    barrier = pltpu.get_barrier_semaphore()
    for k in range(1, members):
        target = lax.rem(place + k, members)
        pl.semaphore_signal(
            barrier,
            inc=1,
            device_id={"region": target // 2, "pno": lax.rem(target, 2)},
            device_id_type=MESH,
        )
    for k in range(1, peers):
        pl.semaphore_signal(
            barrier, inc=1, device_id={"aux": lax.rem(mine + k, peers)}, device_id_type=MESH
        )
    own_amplitudes = pltpu.make_async_copy(
        amplitudes_ref, nearby.at[pl.ds(pairs, pairs)], own_sem
    )
    own_amplitudes.start()
    pl.semaphore_wait(barrier, members - 1 + peers - 1)

    def remote(src, dst, send, recv, device):
        return pltpu.make_async_remote_copy(
            src_ref=src,
            dst_ref=dst,
            send_sem=send,
            recv_sem=recv,
            device_id=device,
            device_id_type=MESH,
        )

    ahead = (z + 1, z - 1)
    ahead_exists = (z < regions - 1, z > 0)
    ahead_is_end = (z == regions - 2, z == 1)
    ahead_goes_on = (z < regions - 2, z > 1)
    at_end = (z == regions - 1, z == 0)

    def source(d, e):
        region = z - 1 - e // occ if d == 0 else z + 1 + e // occ
        return region, (region >= 0) & (region < regions), region * occ + lax.rem(e, occ)

    def own_copy(d, o):
        return remote(
            rows_ref.at[o, row_part],
            far_rows.at[z * occ + o, row_part],
            link_send.at[d, o],
            link_recv.at[d, o],
            {"region": ahead[d]},
        )

    def onward_copy(d, e, orbital):
        return remote(
            far_rows.at[orbital, row_part],
            far_rows.at[orbital, row_part],
            link_send.at[d, e + occ],
            link_recv.at[d, e + occ],
            {"region": ahead[d]},
        )

    def rows_to_core(d, e, orbital, which):
        return remote(
            far_rows.at[orbital, which],
            far_rows.at[orbital, which],
            core_send.at[d, e],
            core_recv.at[d, e],
            sibling,
        )

    def gram_to_core(d, e, orbital, which):
        return remote(
            gram.at[orbital, :, which],
            gram.at[orbital, :, which],
            core_send.at[d, e],
            core_recv.at[d, e],
            sibling,
        )

    def edge_copy(d, e, orbital):
        slot = lax.rem(e, slots)
        return remote(
            edge_gram.at[slot, :, gram_part],
            gram.at[orbital, :, gram_part],
            edge_send.at[slot],
            link_recv.at[d, e + occ],
            {"region": ahead[d]},
        )

    def maps_copy():
        return remote(
            maps_ref.at[:, 1],
            second_maps.at[:, :, own_columns],
            maps_send,
            maps_recv,
            sibling,
        )

    def halo_copy(d):
        return remote(
            nearby.at[pl.ds(pairs + mine * share, share)],
            nearby.at[pl.ds((0 if d == 0 else 2) * pairs + mine * share, share)],
            halo_send.at[d],
            halo_recv.at[d],
            {"region": ahead[d]},
        )

    def share_copy(d, k, origin):
        block = nearby.at[pl.ds((0 if d == 0 else 2) * pairs + origin * share, share)]
        return remote(
            block,
            block,
            share_send.at[d, k - 1],
            share_recv.at[d, k - 1],
            {"aux": lax.rem(mine + k, peers)},
        )

    behind_exists = (z > 0, z < regions - 1)

    for d in range(2):

        @pl.when(ahead_exists[d])
        def _(d=d):
            for o in range(DEPTH):
                own_copy(d, o).start()

        @pl.when(jnp.logical_not(behind_exists[d]))
        def _(d=d):
            nearby[pl.ds((0 if d == 0 else 2) * pairs, pairs)] = jnp.zeros(
                (pairs, columns, width), BF16
            )

    maps_copy().start()
    for o in range(occ):
        own_t[o] = rows_ref[o].T

    def own_gram(o, carry):
        for i in range(occ):
            gram[z * occ + o, i] = jnp.dot(
                own_t[i], rows_ref[o], preferred_element_type=F32
            ).astype(BF16)
        return carry

    lax.fori_loop(0, occ, own_gram, 0)

    def prepare_maps(p, carry):
        first_t[p] = maps_ref[p, 0].T
        second_maps[p, :, own_columns] = maps_ref[p, 1]
        return carry

    lax.fori_loop(0, pairs, prepare_maps, 0)
    own_amplitudes.wait()

    def edge_step(d, e):
        region, valid, orbital = source(d, e)

        @pl.when(valid)
        def _():
            @pl.when(e >= slots)
            def _():
                edge_copy(d, e, orbital).wait_send()

            for i in range(occ):
                edge_gram[lax.rem(e, slots), i] = jnp.dot(
                    edge_t[i], far_rows[orbital], preferred_element_type=F32
                ).astype(BF16)
            edge_copy(d, e, orbital).start()

    def in_queue(d, k, act):
        @pl.when(ahead_exists[d] & (k < occ))
        def _():
            act(own_copy(d, k))

        region, valid, orbital = source(d, k - occ)

        @pl.when(ahead_goes_on[d] & valid & (k >= occ))
        def _():
            act(onward_copy(d, k - occ, orbital))

    def queue_step(d, e):
        in_queue(d, e, lambda copy: copy.wait_send())
        in_queue(d, e + DEPTH, lambda copy: copy.start())

    def step(e, carry):
        for d in range(2):
            region, valid, orbital = source(d, e)
            is_gram = at_end[d] & (e >= occ)

            @pl.when(valid & jnp.logical_not(is_gram))
            def _(d=d, orbital=orbital):
                onward_copy(d, e - occ, orbital).wait_recv()
                rows_to_core(d, e, orbital, row_part).start()

            @pl.when(valid & is_gram)
            def _(d=d, orbital=orbital):
                remote(
                    gram.at[orbital, :, gram_part],
                    gram.at[orbital, :, gram_part],
                    link_send.at[d, e],
                    link_recv.at[d, e],
                    sibling,
                ).wait_recv()
                gram_to_core(d, e, orbital, gram_part).start()

        for d in range(2):

            queue_step(d, e)

            @pl.when(ahead_exists[d] & (e == HALO_STEP))
            def _(d=d):
                halo_copy(d).start()

            @pl.when(behind_exists[d] & (e == SHARE_STEP))
            def _(d=d):
                block = nearby.at[pl.ds((0 if d == 0 else 2) * pairs + mine * share, share)]
                remote(block, block, halo_send.at[d], halo_recv.at[d], sibling).wait_recv()
                for k in range(1, peers):
                    share_copy(d, k, mine).start()

        for d in range(2):
            region, valid, orbital = source(d, e)
            is_gram = at_end[d] & (e >= occ)

            @pl.when(valid & jnp.logical_not(is_gram))
            def _(d=d, orbital=orbital):
                rows_to_core(d, e, orbital, row_rest).wait_recv()

                @pl.when(ahead_is_end[d] & (e >= occ))
                def _():
                    edge_step(d, e)

                for i in range(occ):
                    gram[orbital, i] = jnp.dot(
                        own_t[i], far_rows[orbital], preferred_element_type=F32
                    ).astype(BF16)

            @pl.when(valid & is_gram)
            def _(d=d, orbital=orbital):
                gram_to_core(d, e, orbital, gram_rest).wait_recv()

        for d in range(2):

            @pl.when(ahead_is_end[d] & (e == occ - 1))
            def _(d=d):
                for o in range(occ):
                    edge_t[o] = far_rows[ahead[d] * occ + o].T

                def first_edges(k, inner):
                    edge_step(d, k)
                    return inner

                lax.fori_loop(0, occ, first_edges, 0)

        return carry

    lax.fori_loop(0, steps, step, 0)

    remote(
        maps_ref.at[:, 1],
        second_maps.at[:, :, pl.ds(pl.multiple_of((1 - core) * columns, columns), columns)],
        maps_send,
        maps_recv,
        sibling,
    ).wait_recv()

    def peer_copy(k, c):
        block = pl.ds(c * CHUNK, CHUNK)
        return remote(
            partials.at[mine, block],
            partials.at[mine, block],
            peer_send.at[k - 1, c],
            peer_recv.at[k - 1, c],
            {"aux": lax.rem(mine + k, peers)},
        )

    def project(c, carry):
        for q in range(CHUNK):
            p = c * CHUNK + q
            first = jnp.clip(whole_ref[2 * p] - z * occ, 0, occ - 1)
            matrix = gram[whole_ref[2 * p + 1], first]
            turned = jnp.dot(first_t[p], matrix, preferred_element_type=F32).astype(BF16)
            block = jnp.dot(turned, second_maps[p], preferred_element_type=F32)
            partials[mine, p] = block.astype(BF16)
        for k in range(1, peers):
            peer_copy(k, c).start()
        return carry

    lax.fori_loop(0, pairs // CHUNK, project, 0)

    for d in range(2):

        @pl.when(behind_exists[d])
        def _(d=d):
            for k in range(1, peers):
                share_copy(d, k, mine).wait_send()
                share_copy(d, k, lax.rem(mine - k + peers, peers)).wait_recv()

    row_ids = core * columns + lax.broadcasted_iota(jnp.int32, (columns, width), 0)
    col_ids = lax.broadcasted_iota(jnp.int32, (columns, width), 1)
    last_ids = jnp.maximum(row_ids, col_ids)
    orbital_ids = lax.broadcasted_iota(
        jnp.int32, spread.shape, 0
    ) * occ + lax.broadcasted_iota(jnp.int32, spread.shape, 1)
    held = lax.broadcasted_iota(jnp.int32, spread.shape, 1) < occ
    orbital_ids = jnp.where(held, orbital_ids, -1)
    spread[...] = jnp.zeros_like(spread)
    contract = (((1,), (1,)), ((), ()))

    def collect(c, carry):
        for k in range(1, peers):
            origin = lax.rem(mine - k + peers, peers)
            block = pl.ds(c * CHUNK, CHUNK)
            remote(
                partials.at[origin, block],
                partials.at[origin, block],
                peer_send.at[k - 1, c],
                peer_recv.at[k - 1, c],
                {"aux": lax.rem(mine + k, peers)},
            ).wait_recv()
        for q in range(CHUNK):
            p = c * CHUNK + q
            exchange = partials[0, p].astype(F32)
            for k in range(1, peers):
                exchange = exchange + partials[k, p].astype(F32)
            coupling = jnp.zeros((columns, width), F32)
            factors = couplings_ref[pl.ds(p, 1)]
            for n in range(couplings_ref.shape[1]):
                taken = nearby[jnp.clip(whole_ref[(2 + n) * pairs + p] - (z - 1) * pairs, 0, 3 * pairs - 1)]
                coupling = coupling + factors[:, n : n + 1] * taken.astype(F32)
            first = whole_ref[2 * p]
            second = whole_ref[2 * p + 1]
            occupied = occupied_ref[first] + occupied_ref[second]
            energies = energies_ref[pl.ds(p, 1)]
            own_energies = jnp.where(core == 0, energies[:, :columns], energies[:, columns:])
            row_energy = jnp.broadcast_to(own_energies, (width, columns)).T
            denominator = row_energy + energies - occupied
            update = jnp.where(
                last_ids < counts_ref[p], (coupling - exchange) / denominator, 0.0
            )
            new_ref[p] = update.astype(BF16)
            weight = jnp.sum(update * update, axis=1, keepdims=True) / width
            weight = jnp.broadcast_to(weight, (columns, columns)).T[0:8].astype(BF16)
            for which, orbital in ((0, first), (1, second)):
                vec = lax.dot_general(
                    weight, maps_ref[p, which], contract, preferred_element_type=F32
                )
                spread[...] += jnp.where(orbital_ids == orbital, vec[None], 0.0)
        return carry

    lax.fori_loop(0, pairs // CHUNK, collect, 0)

    def spread_copy(k):
        target = lax.rem(place + k, members)
        return remote(
            spread.at[target // 2],
            gathered.at[place],
            spread_send.at[k - 1],
            spread_recv.at[k - 1],
            {"region": target // 2, "pno": lax.rem(target, 2)},
        )

    for k in range(1, members):
        spread_copy(k).start()
    gathered[place] = spread[z]

    def drain(e, carry):
        for d in range(2):
            region, valid, orbital = source(d, e)
            is_gram = at_end[d] & (e >= occ)

            @pl.when(valid & jnp.logical_not(is_gram))
            def _(d=d, orbital=orbital):
                rows_to_core(d, e, orbital, row_part).wait_send()

                @pl.when(
                    ahead_is_end[d] & ((e >= (regions - 2) * occ - slots))
                )
                def _():
                    edge_copy(d, e, orbital).wait_send()

            @pl.when(valid & is_gram)
            def _(d=d, orbital=orbital):
                gram_to_core(d, e, orbital, gram_part).wait_send()

        return carry

    lax.fori_loop(0, steps, drain, 0)
    maps_copy().wait_send()

    for d in range(2):

        @pl.when(ahead_exists[d])
        def _(d=d):
            halo_copy(d).wait_send()

    def drain_peers(c, carry):
        for k in range(1, peers):
            peer_copy(k, c).wait_send()
        return carry

    lax.fori_loop(0, pairs // CHUNK, drain_peers, 0)
    for k in range(1, members):
        spread_copy(k).wait_send()
        origin = lax.rem(place - k + members, members)
        remote(
            gathered.at[origin],
            gathered.at[origin],
            spread_send.at[k - 1],
            spread_recv.at[k - 1],
            sibling,
        ).wait_recv()
    total = gathered[0]
    for k in range(1, members):
        total = total + gathered[k]
    density_ref[...] = total[0:occ]


def body(
    three_index,
    pno_maps,
    amplitudes,
    pair_orbitals,
    neighbours,
    couplings,
    pno_energies,
    occ_energies,
    pno_counts,
):
    regions = lax.axis_size("region")
    peers = lax.axis_size("aux")
    occ, aux_rows, virtuals = three_index.shape
    pairs, _, _, columns = pno_maps.shape
    width = columns * lax.axis_size("pno")
    orbitals = regions * occ
    steps = (regions - 1) * occ
    mine = lax.dynamic_slice_in_dim(pair_orbitals, lax.axis_index("region") * pairs, pairs)
    whole = jnp.concatenate([mine.reshape(-1), neighbours.T.reshape(-1)])
    smem = pl.BlockSpec(memory_space=pltpu.SMEM)
    vmem = pl.BlockSpec(memory_space=pltpu.VMEM)
    anywhere = pl.BlockSpec(memory_space=pl.ANY)
    dma = pltpu.SemaphoreType.DMA
    return pl.pallas_call(
        functools.partial(exchange_kernel, regions, peers),
        out_shape=(
            jax.ShapeDtypeStruct((pairs, columns, width), BF16),
            jax.ShapeDtypeStruct((occ, virtuals), F32),
        ),
        in_specs=[smem] * 3 + [vmem] * 4 + [anywhere],
        out_specs=(vmem, vmem),
        scratch_shapes=[
            pltpu.VMEM((occ, virtuals, aux_rows), BF16),
            pltpu.VMEM((occ, virtuals, aux_rows), BF16),
            pltpu.VMEM((orbitals, aux_rows, virtuals), BF16),
            pltpu.VMEM((orbitals, occ, virtuals, virtuals), BF16),
            pltpu.VMEM((2 * occ, occ, virtuals, virtuals), BF16),
            pltpu.VMEM((pairs, virtuals, width), BF16),
            pltpu.VMEM((pairs, columns, virtuals), BF16),
            pltpu.VMEM((peers, pairs, columns, width), BF16),
            pltpu.VMEM((3 * pairs, columns, width), BF16),
            pltpu.VMEM((regions, 8, virtuals), F32),
            pltpu.VMEM((2 * regions, 8, virtuals), F32),
            dma((2, steps)),
            dma((2, steps)),
            dma((2, steps)),
            dma((2, steps)),
            dma((2 * occ,)),
            dma,
            dma,
            dma((peers - 1, pairs // CHUNK)),
            dma((peers - 1, pairs // CHUNK)),
            dma,
            dma((2,)),
            dma((2,)),
            dma((2, peers - 1)),
            dma((2, peers - 1)),
            dma((2 * regions - 1,)),
            dma((2 * regions - 1,)),
        ],
        compiler_params=pltpu.CompilerParams(
            collective_id=0, has_side_effects=True, vmem_limit_bytes=58 * 2**20
        ),
        cost_estimate=pl.CostEstimate(
            flops=10**10, bytes_accessed=150 * 10**6, transcendentals=0
        ),
        name="update",
    )(
        whole,
        occ_energies,
        pno_counts,
        couplings,
        three_index,
        pno_maps,
        pno_energies,
        amplitudes,
    )


def solution(mesh):
    in_specs = (
        P(("parts", "region"), "aux", None),
        P(("parts", "region"), None, None, "pno"),
        P(("parts", "region"), "pno", None),
        P("parts", None),
        P(("parts", "region"), None),
        P(("parts", "region"), None),
        P(("parts", "region"), None),
        P("parts"),
        P(("parts", "region")),
    )
    out_specs = (P(("parts", "region"), "pno", None), P(("parts", "region"), None))
    return jax.shard_map(body, mesh=mesh, in_specs=in_specs, out_specs=out_specs, check_vma=False)
```

```python
import functools

import jax
import jax.numpy as jnp
from jax import lax
from jax.experimental import pallas as pl
from jax.experimental.pallas import tpu as pltpu
from jax.sharding import PartitionSpec as P

MESH = pl.DeviceIdType.MESH
F32 = jnp.float32
BF16 = jnp.bfloat16
CHUNK = 4
DEPTH = 2
SHARE_STEP = 1


def exchange_kernel(
    regions,
    peers,
    whole_ref,
    occupied_ref,
    counts_ref,
    couplings_ref,
    rows_ref,
    maps_ref,
    energies_ref,
    amplitudes_ref,
    new_ref,
    density_ref,
    own_t,
    edge_t,
    far_rows,
    gram,
    edge_gram,
    second_maps,
    first_t,
    partials,
    nearby,
    spread,
    gathered,
    link_send,
    link_recv,
    core_send,
    core_recv,
    edge_send,
    maps_send,
    maps_recv,
    peer_send,
    peer_recv,
    own_sem,
    halo_send,
    halo_recv,
    share_send,
    share_recv,
    spread_send,
    spread_recv,
):
    occ, aux_rows, virtuals = rows_ref.shape
    pairs = maps_ref.shape[0]
    columns = maps_ref.shape[3]
    z = lax.axis_index("region")
    core = lax.axis_index("pno")
    mine = lax.axis_index("aux")
    part = aux_rows // 2
    half = virtuals // 2
    steps = (regions - 1) * occ
    slots = 2 * occ
    row_part = pl.ds(pl.multiple_of(core * part, part), part)
    row_rest = pl.ds(pl.multiple_of((1 - core) * part, part), part)
    gram_part = pl.ds(pl.multiple_of(core * half, half), half)
    gram_rest = pl.ds(pl.multiple_of((1 - core) * half, half), half)
    own_columns = pl.ds(pl.multiple_of(core * columns, columns), columns)
    sibling = {"pno": 1 - core}

    members = 2 * regions
    place = 2 * z + core
    share = pairs // peers
    width = 2 * columns

    barrier = pltpu.get_barrier_semaphore()
    for k in range(1, members):
        target = lax.rem(place + k, members)
        pl.semaphore_signal(
            barrier,
            inc=1,
            device_id={"region": target // 2, "pno": lax.rem(target, 2)},
            device_id_type=MESH,
        )
    for k in range(1, peers):
        pl.semaphore_signal(
            barrier, inc=1, device_id={"aux": lax.rem(mine + k, peers)}, device_id_type=MESH
        )
    own_amplitudes = pltpu.make_async_copy(
        amplitudes_ref, nearby.at[pl.ds(pairs, pairs)], own_sem
    )
    own_amplitudes.start()
    pl.semaphore_wait(barrier, members - 1 + peers - 1)

    def remote(src, dst, send, recv, device):
        return pltpu.make_async_remote_copy(
            src_ref=src,
            dst_ref=dst,
            send_sem=send,
            recv_sem=recv,
            device_id=device,
            device_id_type=MESH,
        )

    ahead = (z + 1, z - 1)
    ahead_exists = (z < regions - 1, z > 0)
    ahead_is_end = (z == regions - 2, z == 1)
    ahead_goes_on = (z < regions - 2, z > 1)
    at_end = (z == regions - 1, z == 0)

    def source(d, e):
        region = z - 1 - e // occ if d == 0 else z + 1 + e // occ
        return region, (region >= 0) & (region < regions), region * occ + lax.rem(e, occ)

    def own_copy(d, o):
        return remote(
            rows_ref.at[o, row_part],
            far_rows.at[z * occ + o, row_part],
            link_send.at[d, o],
            link_recv.at[d, o],
            {"region": ahead[d]},
        )

    def onward_copy(d, e, orbital):
        return remote(
            far_rows.at[orbital, row_part],
            far_rows.at[orbital, row_part],
            link_send.at[d, e + occ],
            link_recv.at[d, e + occ],
            {"region": ahead[d]},
        )

    def rows_to_core(d, e, orbital, which):
        return remote(
            far_rows.at[orbital, which],
            far_rows.at[orbital, which],
            core_send.at[d, e],
            core_recv.at[d, e],
            sibling,
        )

    def gram_to_core(d, e, orbital, which):
        return remote(
            gram.at[orbital, :, which],
            gram.at[orbital, :, which],
            core_send.at[d, e],
            core_recv.at[d, e],
            sibling,
        )

    def edge_copy(d, e, orbital):
        slot = lax.rem(e, slots)
        return remote(
            edge_gram.at[slot, :, gram_part],
            gram.at[orbital, :, gram_part],
            edge_send.at[slot],
            link_recv.at[d, e + occ],
            {"region": ahead[d]},
        )

    def maps_copy():
        return remote(
            maps_ref.at[:, 1],
            second_maps.at[:, :, own_columns],
            maps_send,
            maps_recv,
            sibling,
        )

    def halo_copy(d):
        return remote(
            nearby.at[pl.ds(pairs + mine * share, share)],
            nearby.at[pl.ds((0 if d == 0 else 2) * pairs + mine * share, share)],
            halo_send.at[d],
            halo_recv.at[d],
            {"region": ahead[d]},
        )

    def share_copy(d, k, origin):
        block = nearby.at[pl.ds((0 if d == 0 else 2) * pairs + origin * share, share)]
        return remote(
            block,
            block,
            share_send.at[d, k - 1],
            share_recv.at[d, k - 1],
            {"aux": lax.rem(mine + k, peers)},
        )

    own_amplitudes.wait()
    behind_exists = (z > 0, z < regions - 1)

    for d in range(2):

        @pl.when(ahead_exists[d])
        def _(d=d):
            for o in range(DEPTH):
                own_copy(d, o).start()
            halo_copy(d).start()

        @pl.when(jnp.logical_not(behind_exists[d]))
        def _(d=d):
            nearby[pl.ds((0 if d == 0 else 2) * pairs, pairs)] = jnp.zeros(
                (pairs, columns, width), BF16
            )

    maps_copy().start()
    for o in range(occ):
        own_t[o] = rows_ref[o].T

    def own_gram(o, carry):
        for i in range(occ):
            gram[z * occ + o, i] = jnp.dot(
                own_t[i], rows_ref[o], preferred_element_type=F32
            ).astype(BF16)
        return carry

    lax.fori_loop(0, occ, own_gram, 0)

    def prepare_maps(p, carry):
        first_t[p] = maps_ref[p, 0].T
        second_maps[p, :, own_columns] = maps_ref[p, 1]
        return carry

    lax.fori_loop(0, pairs, prepare_maps, 0)

    def edge_step(d, e):
        region, valid, orbital = source(d, e)

        @pl.when(valid)
        def _():
            @pl.when(e >= slots)
            def _():
                edge_copy(d, e, orbital).wait_send()

            for i in range(occ):
                edge_gram[lax.rem(e, slots), i] = jnp.dot(
                    edge_t[i], far_rows[orbital], preferred_element_type=F32
                ).astype(BF16)
            edge_copy(d, e, orbital).start()

    def in_queue(d, k, act):
        @pl.when(ahead_exists[d] & (k < occ))
        def _():
            act(own_copy(d, k))

        region, valid, orbital = source(d, k - occ)

        @pl.when(ahead_goes_on[d] & valid & (k >= occ))
        def _():
            act(onward_copy(d, k - occ, orbital))

    def queue_step(d, e):
        in_queue(d, e, lambda copy: copy.wait_send())
        in_queue(d, e + DEPTH, lambda copy: copy.start())

    def step(e, carry):
        for d in range(2):
            region, valid, orbital = source(d, e)
            is_gram = at_end[d] & (e >= occ)

            @pl.when(valid & jnp.logical_not(is_gram))
            def _(d=d, orbital=orbital):
                onward_copy(d, e - occ, orbital).wait_recv()
                rows_to_core(d, e, orbital, row_part).start()

            @pl.when(valid & is_gram)
            def _(d=d, orbital=orbital):
                remote(
                    gram.at[orbital, :, gram_part],
                    gram.at[orbital, :, gram_part],
                    link_send.at[d, e],
                    link_recv.at[d, e],
                    sibling,
                ).wait_recv()
                gram_to_core(d, e, orbital, gram_part).start()

        for d in range(2):

            queue_step(d, e)

            @pl.when(behind_exists[d] & (e == SHARE_STEP))
            def _(d=d):
                block = nearby.at[pl.ds((0 if d == 0 else 2) * pairs + mine * share, share)]
                remote(block, block, halo_send.at[d], halo_recv.at[d], sibling).wait_recv()
                for k in range(1, peers):
                    share_copy(d, k, mine).start()

        for d in range(2):
            region, valid, orbital = source(d, e)
            is_gram = at_end[d] & (e >= occ)

            @pl.when(valid & jnp.logical_not(is_gram))
            def _(d=d, orbital=orbital):
                rows_to_core(d, e, orbital, row_rest).wait_recv()

                @pl.when(ahead_is_end[d] & (e >= occ))
                def _():
                    edge_step(d, e)

                for i in range(occ):
                    gram[orbital, i] = jnp.dot(
                        own_t[i], far_rows[orbital], preferred_element_type=F32
                    ).astype(BF16)

            @pl.when(valid & is_gram)
            def _(d=d, orbital=orbital):
                gram_to_core(d, e, orbital, gram_rest).wait_recv()

        for d in range(2):

            @pl.when(ahead_is_end[d] & (e == occ - 1))
            def _(d=d):
                for o in range(occ):
                    edge_t[o] = far_rows[ahead[d] * occ + o].T

                def first_edges(k, inner):
                    edge_step(d, k)
                    return inner

                lax.fori_loop(0, occ, first_edges, 0)

        return carry

    lax.fori_loop(0, steps, step, 0)

    remote(
        maps_ref.at[:, 1],
        second_maps.at[:, :, pl.ds(pl.multiple_of((1 - core) * columns, columns), columns)],
        maps_send,
        maps_recv,
        sibling,
    ).wait_recv()

    def peer_copy(k, c):
        block = pl.ds(c * CHUNK, CHUNK)
        return remote(
            partials.at[mine, block],
            partials.at[mine, block],
            peer_send.at[k - 1, c],
            peer_recv.at[k - 1, c],
            {"aux": lax.rem(mine + k, peers)},
        )

    def project(c, carry):
        for q in range(CHUNK):
            p = c * CHUNK + q
            first = jnp.clip(whole_ref[2 * p] - z * occ, 0, occ - 1)
            matrix = gram[whole_ref[2 * p + 1], first]
            turned = jnp.dot(first_t[p], matrix, preferred_element_type=F32).astype(BF16)
            block = jnp.dot(turned, second_maps[p], preferred_element_type=F32)
            partials[mine, p] = block.astype(BF16)
        for k in range(1, peers):
            peer_copy(k, c).start()
        return carry

    lax.fori_loop(0, pairs // CHUNK, project, 0)

    for d in range(2):

        @pl.when(behind_exists[d])
        def _(d=d):
            for k in range(1, peers):
                share_copy(d, k, mine).wait_send()
                share_copy(d, k, lax.rem(mine - k + peers, peers)).wait_recv()

    row_ids = core * columns + lax.broadcasted_iota(jnp.int32, (columns, width), 0)
    col_ids = lax.broadcasted_iota(jnp.int32, (columns, width), 1)
    last_ids = jnp.maximum(row_ids, col_ids)
    orbital_ids = lax.broadcasted_iota(
        jnp.int32, spread.shape, 0
    ) * occ + lax.broadcasted_iota(jnp.int32, spread.shape, 1)
    held = lax.broadcasted_iota(jnp.int32, spread.shape, 1) < occ
    orbital_ids = jnp.where(held, orbital_ids, -1)
    spread[...] = jnp.zeros_like(spread)
    contract = (((1,), (1,)), ((), ()))

    def collect(c, carry):
        for k in range(1, peers):
            origin = lax.rem(mine - k + peers, peers)
            block = pl.ds(c * CHUNK, CHUNK)
            remote(
                partials.at[origin, block],
                partials.at[origin, block],
                peer_send.at[k - 1, c],
                peer_recv.at[k - 1, c],
                {"aux": lax.rem(mine + k, peers)},
            ).wait_recv()
        for q in range(CHUNK):
            p = c * CHUNK + q
            exchange = partials[0, p].astype(F32)
            for k in range(1, peers):
                exchange = exchange + partials[k, p].astype(F32)
            coupling = jnp.zeros((columns, width), F32)
            factors = couplings_ref[pl.ds(p, 1)]
            for n in range(couplings_ref.shape[1]):
                taken = nearby[jnp.clip(whole_ref[(2 + n) * pairs + p] - (z - 1) * pairs, 0, 3 * pairs - 1)]
                coupling = coupling + factors[:, n : n + 1] * taken.astype(F32)
            first = whole_ref[2 * p]
            second = whole_ref[2 * p + 1]
            occupied = occupied_ref[first] + occupied_ref[second]
            energies = energies_ref[pl.ds(p, 1)]
            own_energies = jnp.where(core == 0, energies[:, :columns], energies[:, columns:])
            row_energy = jnp.broadcast_to(own_energies, (width, columns)).T
            denominator = row_energy + energies - occupied
            update = jnp.where(
                last_ids < counts_ref[p], (coupling - exchange) / denominator, 0.0
            )
            new_ref[p] = update.astype(BF16)
            weight = jnp.sum(update * update, axis=1, keepdims=True) / width
            weight = jnp.broadcast_to(weight, (columns, columns)).T[0:8].astype(BF16)
            for which, orbital in ((0, first), (1, second)):
                vec = lax.dot_general(
                    weight, maps_ref[p, which], contract, preferred_element_type=F32
                )
                spread[...] += jnp.where(orbital_ids == orbital, vec[None], 0.0)
        return carry

    lax.fori_loop(0, pairs // CHUNK, collect, 0)

    def spread_copy(k):
        target = lax.rem(place + k, members)
        return remote(
            spread.at[target // 2],
            gathered.at[place],
            spread_send.at[k - 1],
            spread_recv.at[k - 1],
            {"region": target // 2, "pno": lax.rem(target, 2)},
        )

    for k in range(1, members):
        spread_copy(k).start()
    gathered[place] = spread[z]

    def drain(e, carry):
        for d in range(2):
            region, valid, orbital = source(d, e)
            is_gram = at_end[d] & (e >= occ)

            @pl.when(valid & jnp.logical_not(is_gram))
            def _(d=d, orbital=orbital):
                rows_to_core(d, e, orbital, row_part).wait_send()

                @pl.when(
                    ahead_is_end[d] & ((e >= (regions - 2) * occ - slots))
                )
                def _():
                    edge_copy(d, e, orbital).wait_send()

            @pl.when(valid & is_gram)
            def _(d=d, orbital=orbital):
                gram_to_core(d, e, orbital, gram_part).wait_send()

        return carry

    lax.fori_loop(0, steps, drain, 0)
    maps_copy().wait_send()

    for d in range(2):

        @pl.when(ahead_exists[d])
        def _(d=d):
            halo_copy(d).wait_send()

    def drain_peers(c, carry):
        for k in range(1, peers):
            peer_copy(k, c).wait_send()
        return carry

    lax.fori_loop(0, pairs // CHUNK, drain_peers, 0)
    for k in range(1, members):
        spread_copy(k).wait_send()
        origin = lax.rem(place - k + members, members)
        remote(
            gathered.at[origin],
            gathered.at[origin],
            spread_send.at[k - 1],
            spread_recv.at[k - 1],
            sibling,
        ).wait_recv()
    total = gathered[0]
    for k in range(1, members):
        total = total + gathered[k]
    density_ref[...] = total[0:occ]


def body(
    three_index,
    pno_maps,
    amplitudes,
    pair_orbitals,
    neighbours,
    couplings,
    pno_energies,
    occ_energies,
    pno_counts,
):
    regions = lax.axis_size("region")
    peers = lax.axis_size("aux")
    occ, aux_rows, virtuals = three_index.shape
    pairs, _, _, columns = pno_maps.shape
    width = columns * lax.axis_size("pno")
    orbitals = regions * occ
    steps = (regions - 1) * occ
    mine = lax.dynamic_slice_in_dim(pair_orbitals, lax.axis_index("region") * pairs, pairs)
    whole = jnp.concatenate([mine.reshape(-1), neighbours.T.reshape(-1)])
    smem = pl.BlockSpec(memory_space=pltpu.SMEM)
    vmem = pl.BlockSpec(memory_space=pltpu.VMEM)
    anywhere = pl.BlockSpec(memory_space=pl.ANY)
    dma = pltpu.SemaphoreType.DMA
    return pl.pallas_call(
        functools.partial(exchange_kernel, regions, peers),
        out_shape=(
            jax.ShapeDtypeStruct((pairs, columns, width), BF16),
            jax.ShapeDtypeStruct((occ, virtuals), F32),
        ),
        in_specs=[smem] * 3 + [vmem] * 4 + [anywhere],
        out_specs=(vmem, vmem),
        scratch_shapes=[
            pltpu.VMEM((occ, virtuals, aux_rows), BF16),
            pltpu.VMEM((occ, virtuals, aux_rows), BF16),
            pltpu.VMEM((orbitals, aux_rows, virtuals), BF16),
            pltpu.VMEM((orbitals, occ, virtuals, virtuals), BF16),
            pltpu.VMEM((2 * occ, occ, virtuals, virtuals), BF16),
            pltpu.VMEM((pairs, virtuals, width), BF16),
            pltpu.VMEM((pairs, columns, virtuals), BF16),
            pltpu.VMEM((peers, pairs, columns, width), BF16),
            pltpu.VMEM((3 * pairs, columns, width), BF16),
            pltpu.VMEM((regions, 8, virtuals), F32),
            pltpu.VMEM((2 * regions, 8, virtuals), F32),
            dma((2, steps)),
            dma((2, steps)),
            dma((2, steps)),
            dma((2, steps)),
            dma((2 * occ,)),
            dma,
            dma,
            dma((peers - 1, pairs // CHUNK)),
            dma((peers - 1, pairs // CHUNK)),
            dma,
            dma((2,)),
            dma((2,)),
            dma((2, peers - 1)),
            dma((2, peers - 1)),
            dma((2 * regions - 1,)),
            dma((2 * regions - 1,)),
        ],
        compiler_params=pltpu.CompilerParams(
            collective_id=0, has_side_effects=True, vmem_limit_bytes=58 * 2**20
        ),
        cost_estimate=pl.CostEstimate(
            flops=10**10, bytes_accessed=150 * 10**6, transcendentals=0
        ),
        name="update",
    )(
        whole,
        occ_energies,
        pno_counts,
        couplings,
        three_index,
        pno_maps,
        pno_energies,
        amplitudes,
    )


def solution(mesh):
    in_specs = (
        P(("parts", "region"), "aux", None),
        P(("parts", "region"), None, None, "pno"),
        P(("parts", "region"), "pno", None),
        P("parts", None),
        P(("parts", "region"), None),
        P(("parts", "region"), None),
        P(("parts", "region"), None),
        P("parts"),
        P(("parts", "region")),
    )
    out_specs = (P(("parts", "region"), "pno", None), P(("parts", "region"), None))
    return jax.shard_map(body, mesh=mesh, in_specs=in_specs, out_specs=out_specs, check_vma=False)
```
